1024 devices in a mesh: dp: 16 (over y_hi, x, core), expert: 64 (over z, y_lo).
Axes of the slice: x: 4, y: 8 (y_hi: 2, y_lo: 4; y = y_hi * 4 + y_lo), z: 16, core: 2. Of those that a mesh axis runs over, the one named last changes fastest.
Arguments:
- hidden_acts: bfloat16 [16, 64, 128, 512], P('dp', 'expert'), may hold values from -6 to 6
- token_gradients: bfloat16 [16, 64, 32, 2, 3584], P('dp', 'expert'), may hold values from -0.09375 to 0.09375
- local_hidden: bfloat16 [16, 64, 128, 512], P('dp', 'expert'), may hold values from -6 to 6
- local_grads: bfloat16 [16, 64, 128, 3584], P('dp', 'expert'), may hold values from -0.09375 to 0.09375
- counts: int32 [16, 64, 32], P('dp'), may hold values from 0 to 2, as said below
- weight: float32 [64, 512, 3584], P('expert', 'dp'), may hold values from -0.1875 to 0.1875
- moment: bfloat16 [64, 512, 3584], P('expert', 'dp'), may hold values from -2.5 to 2.5
- second: bfloat16 [64, 512, 3584], P('expert', 'dp'), may hold values from 0.049804688 to 2
Outputs:
- new_weight: float32 [64, 512, 3584], P('expert', 'dp')
- new_moment: bfloat16 [64, 512, 3584], P('expert', 'dp')
- new_second: bfloat16 [64, 512, 3584], P('expert', 'dp')
The draws below stay inside these ranges and needn't reach their ends.
Inputs may be any that keep to these rules, and one draw needn't show every extreme that they name: `counts`: A source fills its slots for an expert from the first on. In every replica each expert has some source with all 2 slots filled, and one expert has all slots of every source filled.
All inputs are finite; a program needn't handle non-finite values.
Results may differ from the reference program's by a relative error of at most 0.009.
Values may be sent and summed in bfloat16 or wider, within the bound.
No kernel may reach another device: no remote copies, remote signals or barrier semaphores. Data moves between devices by JAX's collectives and lax.ppermute only.
A program may use at most 64 MiB of HBM per device.

```python
import math
import jax
import jax.numpy as jnp
from jax import lax

D = 3584
FF = 1024
PAIR = 2
CAP = 128
RES = 128
SLOT = 2
EXPERTS = 32
N_DP = 16
N_EXPERT = 64


def draw_counts(key, part):
    key = jax.random.fold_in(key, 7)
    subkeys = jax.random.split(key, 4)
    hotness = jax.random.randint(subkeys[0], (1, 1, EXPERTS), 0, 4)
    base_fill = jax.random.randint(subkeys[1], (N_DP, N_EXPERT, EXPERTS), 0, SLOT + 1)
    filled = jnp.minimum(base_fill * (hotness + 1) // 2, SLOT)
    full_source = jax.random.randint(subkeys[2], (N_DP, 1, EXPERTS), 0, N_EXPERT)
    source_ids = jnp.arange(N_EXPERT)[None, :, None]
    filled = jnp.where(source_ids == full_source, SLOT, filled)
    full_expert = jax.random.randint(subkeys[3], (N_DP, 1, 1), 0, EXPERTS)
    expert_ids = jnp.arange(EXPERTS)[None, None, :]
    filled = jnp.where(expert_ids == full_expert, SLOT, filled)
    return filled.astype(jnp.int32)


def raised(entries, stream_key, source, target, blocks, factor):
    def block_of(position):
        return (jnp.arange(entries.shape[position]) // (entries.shape[position] // blocks)).reshape((-1,) + (1,) * (entries.ndim - 1 - position))

    first = jax.random.permutation(stream_key, blocks)[block_of(target)]
    far = (block_of(target) + blocks // 2) % blocks
    return jnp.where((block_of(source) == first) | (block_of(source) == far), factor * entries, entries)


def shard_levels(rng, dims, shards, low, top_value):
    gain, own = 1.0, jax.random.fold_in(rng, 6)
    for position, blocks in shards:
        draws = jnp.exp(jax.random.uniform(jax.random.fold_in(own, position), (blocks,), jnp.float32, low / len(shards), top_value / len(shards)))
        gain = gain * jnp.repeat(draws, dims[position] // blocks).reshape([-1 if axis == position else 1 for axis in range(len(dims))])
    return gain


def noise(key, extent, scale, reach, shards=(), held_as=jnp.bfloat16):
    values = jax.random.normal(key, extent, jnp.float32) * scale
    if len(shards) > 0:
        values = shard_levels(key, extent, shards, -0.22, 0.18) * values
    return jnp.clip(values, min=-reach, max=reach).astype(held_as)


def noise_with(own_key, shape, deviation, limit, shards, heavy, kind=jnp.bfloat16):
    entries = deviation * jax.random.normal(own_key, shape, jnp.float32)
    if shards:
        entries = entries * shard_levels(own_key, shape, shards, -0.22, 0.18)
    return jnp.clip(raised(entries, jax.random.fold_in(own_key, 3), *heavy), -limit, limit).astype(kind)


def setup_inputs(seed: int = 0) -> dict:
    keys = jax.random.split(jax.random.key(seed), 9)
    hidden_acts = noise_with(keys[0], (N_DP, N_EXPERT, CAP, FF // PAIR), 1.0, 6.0, ((0, 16), (1, 64)), (0, 3, 16, 2.0))
    token_gradients = noise(keys[1], (N_DP, N_EXPERT, EXPERTS, SLOT, D), (N_DP * (CAP + RES)) ** -0.5, 0.09375, ((0, 16), (1, 64)))
    local_hidden = noise_with(keys[2], (N_DP, N_EXPERT, RES, FF // PAIR), 1.0, 6.0, ((0, 16), (1, 64)), (0, 3, 16, 2.0))
    local_grads = noise(keys[3], (N_DP, N_EXPERT, RES, D), (N_DP * (CAP + RES)) ** -0.5, 0.09375, ((0, 16), (1, 64)))
    counts = draw_counts(jax.random.fold_in(keys[8], 71), 0)
    weight = noise(keys[5], (N_EXPERT, FF // PAIR, D), FF ** -0.5, 0.1875, ((0, 64), (1, 16)), jnp.float32)
    moment = noise(keys[6], (N_EXPERT, FF // PAIR, D), 0.3, 2.5, ((0, 64), (1, 16)))
    second = jnp.clip(jnp.exp(math.log(2.0) - 3.6927934 * jax.random.uniform(keys[7], (N_EXPERT, FF // PAIR, D), jnp.float32) ** shard_levels(keys[7], (N_EXPERT, FF // PAIR, D), ((0, 64), (1, 16)), -0.2, 0.2)), 0.049804688, 2.0).astype(jnp.bfloat16)
    return dict(hidden_acts=hidden_acts, token_gradients=token_gradients, local_hidden=local_hidden, local_grads=local_grads, counts=counts, weight=weight, moment=moment, second=second)


beta_one = 0.9
beta_two = 0.95
learn_rate = 0.00022
decay_rate = 0.1
epsilon = 1e-08
correct_one = 1.0 - 0.9 ** 20
correct_two = 1.0 - 0.95 ** 20

def block_gradient(hidden_acts, token_gradients, local_hidden, local_grads, counts, block_id):
    expert_id = block_id // PAIR
    gradient_row_block = lax.dynamic_index_in_dim(token_gradients, expert_id, axis=2, keepdims=False)
    gradient_row_block = gradient_row_block.reshape(N_DP, CAP, D)
    filled = lax.dynamic_index_in_dim(counts, expert_id, axis=2, keepdims=False)
    slot_ids = jnp.arange(SLOT, dtype=jnp.int32)
    is_live = (slot_ids[None, None, :] < filled[:, :, None]).reshape(N_DP, CAP)
    hidden_state = lax.dynamic_index_in_dim(hidden_acts, block_id, axis=1, keepdims=False)
    hidden_state = jnp.where(is_live[:, :, None], hidden_state, jnp.zeros_like(hidden_state))
    partial_sum_blocks = jnp.einsum('pao,pac->poc', hidden_state.astype(jnp.float32), gradient_row_block.astype(jnp.float32))
    owned_hidden_state = lax.dynamic_index_in_dim(local_hidden, block_id, axis=1, keepdims=False)
    owned_gradients = lax.dynamic_index_in_dim(local_grads, block_id, axis=1, keepdims=False)
    partial_sum_blocks = partial_sum_blocks + jnp.einsum('pao,pac->poc', owned_hidden_state.astype(jnp.float32), owned_gradients.astype(jnp.float32))
    rounded = lax.optimization_barrier(partial_sum_blocks.astype(jnp.bfloat16))
    return lax.optimization_barrier(jnp.sum(rounded.astype(jnp.float32), axis=0))

def adamw_update(gradient, weight, moment, second):
    moment_new = beta_one * moment.astype(jnp.float32) + (1.0 - beta_one) * gradient
    second_new = beta_two * second.astype(jnp.float32) + (1.0 - beta_two) * gradient * gradient
    step_direction = moment_new / correct_one / (jnp.sqrt(second_new / correct_two) + epsilon)
    new_weight = weight - learn_rate * (step_direction + decay_rate * weight)
    return (new_weight, moment_new.astype(jnp.bfloat16), second_new.astype(jnp.bfloat16))

def reference(hidden_acts, token_gradients, local_hidden, local_grads, counts, weight, moment, second):
    blocks = jnp.arange(N_EXPERT, dtype=jnp.int32)
    gradient = lax.map(lambda block_id: block_gradient(hidden_acts, token_gradients, local_hidden, local_grads, counts, block_id), blocks)
    new_weight, new_moment, new_second = adamw_update(gradient, weight, moment, second)
    return (new_weight, new_moment, new_second)
```

```python
import jax
import jax.numpy as jnp
from jax import lax
from jax.sharding import Mesh, PartitionSpec as P

AXES = ("y_hi", "x", "core", "z", "y_half", "y_low")

beta_one = 0.9
beta_two = 0.95
learn_rate = 0.00022
decay_rate = 0.1
epsilon = 1e-08
correct_one = 1.0 - 0.9**20
correct_two = 1.0 - 0.95**20


def contract_rows(left_rows, right_rows):
    return lax.dot_general(
        left_rows, right_rows, (((0,), (0,)), ((), ())), preferred_element_type=jnp.float32
    )


def swap(block, axis, pairs):
    return lax.ppermute(block, axis, pairs + [(b, a) for a, b in pairs])


def flip_if(condition, block, axis):
    return jnp.where(condition, jnp.flip(block, axis), block)


def on_device(
    hidden_acts, token_gradients, local_hidden, local_grads, counts, weight, moment, second
):
    core = lax.axis_index("core")
    low = lax.axis_index("y_low")
    expert_id = lax.axis_index("z") * 2 + lax.axis_index("y_half")
    features = token_gradients.shape[-1]
    n_chunks = 2
    per_core = features // 2
    width = per_core // n_chunks
    n_z = 16
    slots = token_gradients.shape[3]
    units = hidden_acts.shape[-1]

    outgoing = token_gradients[0, 0].reshape(n_z, 2, slots, 2, n_chunks, width)
    arrived = [
        lax.all_to_all(
            outgoing[:, :, :, :, chunk].transpose(3, 0, 1, 2, 4).reshape(-1, slots, width),
            ("core", "z", "y_half"),
            0,
            0,
            tiled=True,
        )
        for chunk in range(n_chunks)
    ]

    filled = lax.dynamic_index_in_dim(counts[0], expert_id, axis=1, keepdims=False)
    slot_ids = jnp.arange(slots, dtype=jnp.int32)
    is_live = (slot_ids[None, :] < filled[:, None]).reshape(-1)
    hidden = hidden_acts[0, 0]
    hidden = jnp.where(is_live[:, None], hidden, jnp.zeros_like(hidden))
    hidden = hidden.reshape(n_z, 2, 2, slots, units)
    hidden = flip_if(low == 1, hidden, 2)
    hidden = hidden.reshape(-1, units)
    both = jnp.concatenate([hidden, local_hidden[0, 0]], axis=0)
    both = both.reshape(-1, 2, 4, units // 8).transpose(0, 2, 1, 3).reshape(-1, units)
    both_other = swap(both, "core", [(0, 1)])
    rows = hidden.shape[0]
    first = jnp.where(core == 0, both[:rows], both_other[:rows])
    last = jnp.where(core == 0, both_other[:rows], both[:rows])
    routed = jnp.stack([first, last]).reshape(2, n_z, 2, 2, slots, units)
    routed = routed.transpose(3, 0, 1, 2, 4, 5).reshape(2 * rows, units)
    owned = jnp.concatenate([both[rows:], both_other[rows:]], axis=0)

    grads = local_grads[0, 0].reshape(-1, 2, per_core)
    grads_other = swap(
        lax.dynamic_index_in_dim(grads, 1 - core, 1, keepdims=False), "core", [(0, 1)]
    )
    grads_mine = lax.dynamic_index_in_dim(grads, core, 1, keepdims=False)
    grads_both = jnp.concatenate([grads_mine, grads_other], axis=0)

    def reduce_chunk(left, right, chunk):
        local = grads_both[:, chunk * width : (chunk + 1) * width]
        partial = contract_rows(left, right) + contract_rows(owned, local)
        partial = partial.astype(jnp.bfloat16).reshape(4, units // 4, width)
        partial = lax.all_to_all(partial, "x", 0, 0, tiled=True)
        summed = jnp.sum(partial.astype(jnp.float32), axis=0).astype(jnp.bfloat16)
        summed = summed.reshape(4, units // 16, width)
        summed = lax.all_to_all(summed, ("y_hi", "core"), 0, 0, tiled=True)
        summed = summed.astype(jnp.float32)
        return summed[:2] + summed[2:]

    grads_summed = []
    for chunk in range(n_chunks):
        near = arrived[chunk].reshape(-1, width)
        far = swap(near, "y_low", [(0, 1)])
        grads_summed.append(
            reduce_chunk(routed, jnp.concatenate([near, far], axis=0), chunk)
        )
    summed = jnp.concatenate(
        [grads_summed[chunk][side] for side in range(2) for chunk in range(n_chunks)], axis=-1
    )
    moment_new = beta_one * moment[0].astype(jnp.float32) + (1.0 - beta_one) * summed
    second_new = beta_two * second[0].astype(jnp.float32) + (1.0 - beta_two) * summed * summed
    step_direction = moment_new / correct_one / (jnp.sqrt(second_new / correct_two) + epsilon)
    master = weight[0]
    new_weight = master - learn_rate * (step_direction + decay_rate * master)
    return (
        new_weight[None],
        moment_new.astype(jnp.bfloat16)[None],
        second_new.astype(jnp.bfloat16)[None],
    )


def solution(mesh):
    dp = ("y_hi", "x", "core")
    expert = ("z", "y_half", "y_low")
    fine = Mesh(mesh.devices.reshape(2, 4, 2, 16, 2, 2), AXES)
    outs = P(expert, dp, None)
    return jax.shard_map(
        on_device,
        mesh=fine,
        in_specs=(
            P(dp, expert, None, None),
            P(dp, expert, None, None, None),
            P(dp, expert, None, None),
            P(dp, expert, None, None),
            P(dp, None, None),
            outs,
            outs,
            outs,
        ),
        out_specs=(outs, outs, outs),
        check_vma=False,
    )
```

```python
import jax
import jax.numpy as jnp
from jax import lax
from jax.sharding import Mesh, PartitionSpec as P

AXES = ("y_hi", "x", "core", "z", "y_half", "y_low")
N_X = 4
TILE = 128

beta_one = 0.9
beta_two = 0.95
learn_rate = 0.00022
decay_rate = 0.1
epsilon = 1e-08
correct_one = 1.0 - 0.9**20
correct_two = 1.0 - 0.95**20


def contract_rows(left_rows, right_rows):
    return lax.dot_general(
        left_rows, right_rows, (((0,), (0,)), ((), ())), preferred_element_type=jnp.float32
    )


def on_device(
    hidden_acts, token_gradients, local_hidden, local_grads, counts, weight, moment, second
):
    x = lax.axis_index("x")
    core = lax.axis_index("core")
    expert_id = lax.axis_index("z") * 2 + lax.axis_index("y_half")
    outgoing = token_gradients[0, 0]
    slots, features = outgoing.shape[1:]
    hidden = hidden_acts[0, 0]
    rows, units = hidden.shape
    span = features // N_X
    width = (span // TILE + 1) // 2 * TILE
    shift = span - width

    arrived = lax.all_to_all(outgoing, ("z", "y_half"), 0, 0, tiled=True)

    filled = lax.dynamic_index_in_dim(counts[0], expert_id, axis=1, keepdims=False)
    slot_ids = jnp.arange(slots, dtype=jnp.int32)
    is_live = (slot_ids[None, :] < filled[:, None]).reshape(rows)
    hidden = jnp.where(is_live[:, None], hidden, jnp.zeros_like(hidden))
    hidden = hidden.reshape(-1, 2, slots, units).transpose(1, 0, 2, 3).reshape(rows, units)
    owned_hidden = local_hidden[0, 0]
    owned_gradients = local_grads[0, 0]

    held = []
    for step in range(N_X):
        start = lax.rem(x + step, N_X) * span
        block = lax.dynamic_slice_in_dim(owned_gradients, start, span, axis=1)
        block = jnp.concatenate([block, hidden, owned_hidden], axis=1)
        if step:
            block = lax.ppermute(block, "x", [(i, (i + step) % N_X) for i in range(N_X)])
        held.append(block)
    held = jnp.stack(held)
    mine = lax.dynamic_slice_in_dim(held[:, :, :span], core * shift, width, axis=2)
    other = lax.dynamic_slice_in_dim(held[:, :, :span], (1 - core) * shift, width, axis=2)
    other = jnp.concatenate([other, held[:, :, span:]], axis=2)
    other = lax.ppermute(other, "core", [(0, 1), (1, 0)])
    left = jnp.concatenate(
        [held[:, :, span + units :].reshape(-1, units), other[:, :, width + units :].reshape(-1, units)]
    )
    right = jnp.concatenate(
        [mine.reshape(-1, width), other[:, :, :width].reshape(-1, width)]
    )
    partial = contract_rows(left, right)

    own = held[:, :, span : span + units]
    far = other[:, :, width : width + units]
    pair = jnp.stack([jnp.where(core == 0, own, far), jnp.where(core == 0, far, own)], axis=1)
    back = jnp.flip(pair, 0)
    twice = jnp.concatenate([back, back])
    routed = lax.dynamic_slice_in_dim(twice, N_X - 1 - x, N_X, axis=0).reshape(-1, units)

    near = arrived.reshape(-1, features)
    blocks = jnp.stack(
        [
            near[:, i * span + j * shift : i * span + j * shift + width]
            for i in range(N_X)
            for j in range(2)
            for _ in range(2)
        ]
    )
    gathered = lax.all_to_all(blocks, ("x", "core", "y_low"), 0, 0, tiled=True)
    partial = partial + contract_rows(routed, gathered.reshape(-1, width))

    partial = partial.astype(jnp.bfloat16).reshape(4 * N_X, -1, width)
    partial = lax.all_to_all(partial, ("y_hi", "x", "core"), 0, 0, tiled=True)
    partial = partial.astype(jnp.float32).reshape(2, N_X, 2, -1, width)
    summed = partial[0] + partial[1]
    summed = jnp.concatenate(
        [
            part
            for i in range(N_X)
            for part in (summed[i, 0], summed[i, 1][:, 2 * width - span :])
        ],
        axis=1,
    )
    moment_new = beta_one * moment[0].astype(jnp.float32) + (1.0 - beta_one) * summed
    second_new = beta_two * second[0].astype(jnp.float32) + (1.0 - beta_two) * summed * summed
    step_direction = moment_new / correct_one / (jnp.sqrt(second_new / correct_two) + epsilon)
    master = weight[0]
    new_weight = master - learn_rate * (step_direction + decay_rate * master)
    return (
        new_weight[None],
        moment_new.astype(jnp.bfloat16)[None],
        second_new.astype(jnp.bfloat16)[None],
    )


def solution(mesh):
    dp = ("y_hi", "x", "core")
    expert = ("z", "y_half", "y_low")
    fine = Mesh(mesh.devices.reshape(2, N_X, 2, 16, 2, 2), AXES)
    outs = P(expert, dp, None)
    return jax.shard_map(
        on_device,
        mesh=fine,
        in_specs=(
            P(dp, expert, None, None),
            P(dp, expert, None, None, None),
            P(dp, expert, None, None),
            P(dp, expert, None, None),
            P(dp, None, None),
            outs,
            outs,
            outs,
        ),
        out_specs=(outs, outs, outs),
        check_vma=False,
    )
```

```python
import jax
import jax.numpy as jnp
from jax import lax
from jax.experimental import pallas as pl
from jax.experimental.pallas import tpu as pltpu
from jax.sharding import Mesh, PartitionSpec as P

AXES = ("y_hi", "x", "core", "z", "y_half", "y_low")
N_X = 4
TILE = 128

beta_one = 0.9
beta_two = 0.95
learn_rate = 0.00022
decay_rate = 0.1
epsilon = 1e-08
correct_one = 1.0 - 0.9**20
correct_two = 1.0 - 0.95**20


def contract_rows(left_rows, right_rows):
    return lax.dot_general(
        left_rows, right_rows, (((0,), (0,)), ((), ())), preferred_element_type=jnp.float32
    )


def column_blocks(near, span):
    rows = near.shape[0]

    def kernel(near_ref, out_ref):
        for i in range(N_X):
            block = near_ref[:, i * span : (i + 1) * span]
            for j in range(2):
                out_ref[2 * i + j] = block

    return pl.pallas_call(
        kernel,
        out_shape=jax.ShapeDtypeStruct((2 * N_X, rows, span), near.dtype),
        in_specs=[pl.BlockSpec(memory_space=pltpu.VMEM)],
        out_specs=pl.BlockSpec(memory_space=pltpu.VMEM),
    )(near)


def adamw(sums, weight, moment, second):
    rows, features = weight.shape[1:]
    width = sums.shape[-1]
    span = features // N_X

    def kernel(sums_ref, weight_ref, moment_ref, second_ref, new_weight, new_moment, new_second):
        for j in range(2):
            skip = j * (2 * width - span)
            cols = slice(j * width, j * width + width - skip)
            summed = sums_ref[0, 0, j, :, skip:].astype(jnp.float32)
            summed = summed + sums_ref[1, 0, j, :, skip:].astype(jnp.float32)
            first = beta_one * moment_ref[0, :, cols].astype(jnp.float32)
            first = first + (1.0 - beta_one) * summed
            next_ = beta_two * second_ref[0, :, cols].astype(jnp.float32)
            next_ = next_ + (1.0 - beta_two) * summed * summed
            direction = first / correct_one / (jnp.sqrt(next_ / correct_two) + epsilon)
            master = weight_ref[0, :, cols]
            new_weight[0, :, cols] = master - learn_rate * (direction + decay_rate * master)
            new_moment[0, :, cols] = first.astype(jnp.bfloat16)
            new_second[0, :, cols] = next_.astype(jnp.bfloat16)

    shard = pl.BlockSpec((1, rows, span), lambda i: (0, 0, i))
    return pl.pallas_call(
        kernel,
        grid=(N_X,),
        out_shape=tuple(jax.ShapeDtypeStruct(a.shape, a.dtype) for a in (weight, moment, second)),
        in_specs=[
            pl.BlockSpec((2, 1, 2, rows, width), lambda i: (0, i, 0, 0, 0)),
            shard,
            shard,
            shard,
        ],
        out_specs=(shard, shard, shard),
    )(sums, weight, moment, second)


def on_device(
    hidden_acts, token_gradients, local_hidden, local_grads, counts, weight, moment, second
):
    x = lax.axis_index("x")
    core = lax.axis_index("core")
    expert_id = lax.axis_index("z") * 2 + lax.axis_index("y_half")
    outgoing = token_gradients[0, 0]
    slots, features = outgoing.shape[1:]
    hidden = hidden_acts[0, 0]
    rows, units = hidden.shape
    span = features // N_X
    width = (span // TILE + 1) // 2 * TILE
    shift = span - width

    arrived = lax.all_to_all(outgoing, ("z", "y_half"), 0, 0, tiled=True)

    filled = lax.dynamic_index_in_dim(counts[0], expert_id, axis=1, keepdims=False)
    slot_ids = jnp.arange(slots, dtype=jnp.int32)
    is_live = (slot_ids[None, :] < filled[:, None]).reshape(rows)
    hidden = jnp.where(is_live[:, None], hidden, jnp.zeros_like(hidden))
    hidden = hidden.reshape(-1, 2, slots, units).transpose(1, 0, 2, 3).reshape(rows, units)
    owned_hidden = local_hidden[0, 0]
    owned_gradients = local_grads[0, 0]

    held = []
    for step in range(N_X):
        start = lax.rem(x + step, N_X) * span
        block = lax.dynamic_slice_in_dim(owned_gradients, start, span, axis=1)
        held.append(jnp.concatenate([block, hidden, owned_hidden], axis=1))
    for step in (2, 1, 3):
        held[step] = lax.ppermute(
            held[step], "x", [(i, (i + step) % N_X) for i in range(N_X)]
        )

    blocks = column_blocks(arrived.reshape(-1, features), span)
    held, _ = lax.optimization_barrier((held, blocks))
    gathered = lax.all_to_all(blocks, ("x", "y_low"), 0, 0, tiled=True)
    gathered = gathered.reshape(-1, span)

    back = jnp.stack([block[:, span : span + units] for block in held[::-1]])
    twice = jnp.concatenate([back, back])
    routed = lax.dynamic_slice_in_dim(twice, N_X - 1 - x, N_X, axis=0).reshape(-1, units)
    owned = jnp.concatenate([block[:, span + units :] for block in held])
    columns = jnp.concatenate([block[:, :span] for block in held])

    def partial_of(which):
        start = which * shift
        return contract_rows(
            owned, lax.dynamic_slice_in_dim(columns, start, width, axis=1)
        ) + contract_rows(routed, lax.dynamic_slice_in_dim(gathered, start, width, axis=1))

    other = partial_of(1 - core).astype(jnp.bfloat16)
    other = lax.ppermute(other, "core", [(0, 1), (1, 0)])
    partial = partial_of(core) + other.astype(jnp.float32)

    partial = partial.astype(jnp.bfloat16).reshape(4 * N_X, -1, width)
    partial = lax.all_to_all(partial, ("y_hi", "x", "core"), 0, 0, tiled=True)
    return adamw(partial.reshape(2, N_X, 2, -1, width), weight, moment, second)


def solution(mesh):
    dp = ("y_hi", "x", "core")
    expert = ("z", "y_half", "y_low")
    fine = Mesh(mesh.devices.reshape(2, N_X, 2, 16, 2, 2), AXES)
    outs = P(expert, dp, None)
    return jax.shard_map(
        on_device,
        mesh=fine,
        in_specs=(
            P(dp, expert, None, None),
            P(dp, expert, None, None, None),
            P(dp, expert, None, None),
            P(dp, expert, None, None),
            P(dp, None, None),
            outs,
            outs,
            outs,
        ),
        out_specs=(outs, outs, outs),
        check_vma=False,
    )
```

```python
import jax
import jax.numpy as jnp
from jax import lax
from jax.experimental import pallas as pl
from jax.experimental.pallas import tpu as pltpu
from jax.sharding import Mesh, PartitionSpec as P

AXES = ("y_hi", "x", "core", "z", "y_half", "y_low")
N_X = 4
OWNED = 32
KERNEL_VMEM = 8 * 2**20

beta_one = 0.9
beta_two = 0.95
learn_rate = 0.00022
decay_rate = 0.1
epsilon = 1e-08
correct_one = 1.0 - 0.9**20
correct_two = 1.0 - 0.95**20


def contract_rows(left_rows, right_rows):
    return lax.dot_general(
        left_rows, right_rows, (((0,), (0,)), ((), ())), preferred_element_type=jnp.float32
    )


def column_blocks(near, span):
    rows = near.shape[0]

    def kernel(near_ref, out_ref):
        for i in range(N_X):
            block = near_ref[:, i * span : (i + 1) * span]
            for j in range(2):
                out_ref[2 * i + j] = block

    return pl.pallas_call(
        kernel,
        out_shape=jax.ShapeDtypeStruct((2 * N_X, rows, span), near.dtype),
        in_specs=[pl.BlockSpec(memory_space=pltpu.VMEM)],
        out_specs=pl.BlockSpec(memory_space=pltpu.VMEM),
        compiler_params=pltpu.CompilerParams(vmem_limit_bytes=KERNEL_VMEM),
    )(near)


def adamw(sums, weight, moment, second):
    span = sums.shape[-1]

    def kernel(sums_ref, weight_ref, moment_ref, second_ref, new_weight, new_moment, new_second):
        for i in range(N_X):
            cols = slice(i * span, (i + 1) * span)
            summed = sums_ref[i].astype(jnp.float32) + sums_ref[N_X + i].astype(jnp.float32)
            first = beta_one * moment_ref[0, :, cols].astype(jnp.float32)
            first = first + (1.0 - beta_one) * summed
            next_ = beta_two * second_ref[0, :, cols].astype(jnp.float32)
            next_ = next_ + (1.0 - beta_two) * summed * summed
            direction = first / correct_one / (jnp.sqrt(next_ / correct_two) + epsilon)
            master = weight_ref[0, :, cols]
            new_weight[0, :, cols] = master - learn_rate * (direction + decay_rate * master)
            new_moment[0, :, cols] = first.astype(jnp.bfloat16)
            new_second[0, :, cols] = next_.astype(jnp.bfloat16)

    vmem = pl.BlockSpec(memory_space=pltpu.VMEM)
    return pl.pallas_call(
        kernel,
        out_shape=tuple(jax.ShapeDtypeStruct(a.shape, a.dtype) for a in (weight, moment, second)),
        in_specs=[vmem] * 4,
        out_specs=(vmem,) * 3,
        compiler_params=pltpu.CompilerParams(vmem_limit_bytes=KERNEL_VMEM),
    )(sums, weight, moment, second)


def on_device(
    hidden_acts, token_gradients, local_hidden, local_grads, counts, weight, moment, second
):
    x = lax.axis_index("x")
    core = lax.axis_index("core")
    expert_id = lax.axis_index("z") * 2 + lax.axis_index("y_half")
    outgoing = token_gradients[0, 0]
    slots, features = outgoing.shape[1:]
    hidden = hidden_acts[0, 0]
    rows, units = hidden.shape
    span = features // N_X
    share = units // 2

    arrived = lax.all_to_all(outgoing, ("z", "y_half"), 0, 0, tiled=True)

    filled = lax.dynamic_index_in_dim(counts[0], expert_id, axis=1, keepdims=False)
    slot_ids = jnp.arange(slots, dtype=jnp.int32)
    is_live = (slot_ids[None, :] < filled[:, None]).reshape(rows)
    hidden = jnp.where(is_live[:, None], hidden, jnp.zeros_like(hidden))
    hidden = hidden.reshape(-1, 2, slots, units).transpose(1, 0, 2, 3).reshape(rows, units)
    owned_hidden = local_hidden[0, 0]
    owned_gradients = local_grads[0, 0]

    held = []
    for step in range(N_X):
        start = lax.rem(x + step, N_X) * span
        block = lax.dynamic_slice_in_dim(owned_gradients, start, span, axis=1)
        held.append(jnp.concatenate([block, hidden, owned_hidden], axis=1))
    for step in (2, 1, 3):
        held[step] = lax.ppermute(
            held[step], "x", [(i, (i + step) % N_X) for i in range(N_X)]
        )

    blocks = column_blocks(arrived.reshape(-1, features), span)
    held, _ = lax.optimization_barrier((held, blocks))
    gathered = lax.all_to_all(blocks, ("x", "y_low"), 0, 0, tiled=True)
    gathered = gathered.reshape(-1, span)

    def by_core(rows_of_units):
        split = rows_of_units.reshape(-1, units // (2 * OWNED), 2, OWNED)
        return split.transpose(0, 2, 1, 3).reshape(-1, units)

    back = jnp.stack([block[:, span : span + units] for block in held[::-1]])
    twice = jnp.concatenate([back, back])
    routed = lax.dynamic_slice_in_dim(twice, N_X - 1 - x, N_X, axis=0).reshape(-1, units)
    routed = by_core(routed)
    owned = by_core(jnp.concatenate([block[:, span + units :] for block in held]))
    columns = jnp.concatenate([block[:, :span] for block in held])

    def partial_of(which):
        start = which * share
        return contract_rows(
            lax.dynamic_slice_in_dim(owned, start, share, axis=1), columns
        ) + contract_rows(lax.dynamic_slice_in_dim(routed, start, share, axis=1), gathered)

    other = partial_of(1 - core).astype(jnp.bfloat16)
    other = lax.ppermute(other, "core", [(0, 1), (1, 0)])
    partial = partial_of(core) + other.astype(jnp.float32)

    partial = partial.astype(jnp.bfloat16).reshape(2 * N_X, OWNED, span)
    partial = lax.all_to_all(partial, ("y_hi", "x"), 0, 0, tiled=True)
    return adamw(partial, weight, moment, second)


def solution(mesh):
    dp = ("y_hi", "x", "core")
    expert = ("z", "y_half", "y_low")
    fine = Mesh(mesh.devices.reshape(2, N_X, 2, 16, 2, 2), AXES)
    outs = P(expert, dp, None)
    return jax.shard_map(
        on_device,
        mesh=fine,
        in_specs=(
            P(dp, expert, None, None),
            P(dp, expert, None, None, None),
            P(dp, expert, None, None),
            P(dp, expert, None, None),
            P(dp, None, None),
            outs,
            outs,
            outs,
        ),
        out_specs=(outs, outs, outs),
        check_vma=False,
    )
```

```python
import jax
import jax.numpy as jnp
from jax import lax
from jax.experimental import pallas as pl
from jax.experimental.pallas import tpu as pltpu
from jax.sharding import Mesh, PartitionSpec as P

AXES = ("y_hi", "x", "core", "z", "y_half", "y_low")
N_X = 4
OWNED = 32
KERNEL_VMEM = 8 * 2**20

beta_one = 0.9
beta_two = 0.95
learn_rate = 0.00022
decay_rate = 0.1
epsilon = 1e-08
correct_one = 1.0 - 0.9**20
correct_two = 1.0 - 0.95**20


def contract_rows(left_rows, right_rows):
    return lax.dot_general(
        left_rows, right_rows, (((0,), (0,)), ((), ())), preferred_element_type=jnp.float32
    )


def column_blocks(near, span):
    rows = near.shape[0]

    def kernel(near_ref, out_ref, sems):
        copies = [
            pltpu.make_async_copy(
                near_ref.at[:, i * span : (i + 1) * span], out_ref.at[2 * i + j], sems.at[i, j]
            )
            for i in range(N_X)
            for j in range(2)
        ]
        for copy in copies:
            copy.start()
        for copy in copies:
            copy.wait()

    return pl.pallas_call(
        kernel,
        out_shape=jax.ShapeDtypeStruct((2 * N_X, rows, span), near.dtype),
        in_specs=[pl.BlockSpec(memory_space=pltpu.VMEM)],
        out_specs=pl.BlockSpec(memory_space=pl.ANY),
        scratch_shapes=[pltpu.SemaphoreType.DMA((N_X, 2))],
        compiler_params=pltpu.CompilerParams(vmem_limit_bytes=KERNEL_VMEM),
    )(near)


def adamw(sums, weight, moment, second):
    span = sums.shape[-1]

    rows = weight.shape[1]

    def kernel(sums_ref, weight_ref, moment_ref, second_ref, *rest):
        outs, held, sems = rest[:3], rest[3:6], rest[6]
        copies = []
        for i in range(N_X):
            cols = slice(i * span, (i + 1) * span)
            summed = sums_ref[i].astype(jnp.float32) + sums_ref[N_X + i].astype(jnp.float32)
            first = beta_one * moment_ref[0, :, cols].astype(jnp.float32)
            first = first + (1.0 - beta_one) * summed
            next_ = beta_two * second_ref[0, :, cols].astype(jnp.float32)
            next_ = next_ + (1.0 - beta_two) * summed * summed
            root = jnp.sqrt(next_ * (1.0 / correct_two)) + epsilon
            direction = first * (1.0 / correct_one) / root
            master = weight_ref[0, :, cols]
            held[0][i] = master - learn_rate * (direction + decay_rate * master)
            held[1][i] = first.astype(jnp.bfloat16)
            held[2][i] = next_.astype(jnp.bfloat16)
            for j in range(3):
                copies.append(
                    pltpu.make_async_copy(held[j].at[i], outs[j].at[0, :, cols], sems.at[j, i])
                )
                copies[-1].start()
        for copy in copies:
            copy.wait()

    arrays = (weight, moment, second)
    return pl.pallas_call(
        kernel,
        out_shape=tuple(jax.ShapeDtypeStruct(a.shape, a.dtype) for a in arrays),
        in_specs=[pl.BlockSpec(memory_space=pltpu.VMEM)] * 4,
        out_specs=(pl.BlockSpec(memory_space=pl.ANY),) * 3,
        scratch_shapes=[pltpu.VMEM((N_X, rows, span), a.dtype) for a in arrays]
        + [pltpu.SemaphoreType.DMA((3, N_X))],
        compiler_params=pltpu.CompilerParams(vmem_limit_bytes=KERNEL_VMEM),
    )(sums, *arrays)


def on_device(
    hidden_acts, token_gradients, local_hidden, local_grads, counts, weight, moment, second
):
    x = lax.axis_index("x")
    core = lax.axis_index("core")
    expert_id = lax.axis_index("z") * 2 + lax.axis_index("y_half")
    outgoing = token_gradients[0, 0]
    slots, features = outgoing.shape[1:]
    hidden = hidden_acts[0, 0]
    rows, units = hidden.shape
    span = features // N_X
    share = units // 2

    arrived = lax.all_to_all(outgoing, ("z", "y_half"), 0, 0, tiled=True)

    filled = lax.dynamic_index_in_dim(counts[0], expert_id, axis=1, keepdims=False)
    slot_ids = jnp.arange(slots, dtype=jnp.int32)
    is_live = (slot_ids[None, :] < filled[:, None]).reshape(rows)
    hidden = jnp.where(is_live[:, None], hidden, jnp.zeros_like(hidden))
    hidden = hidden.reshape(-1, 2, slots, units).transpose(1, 0, 2, 3).reshape(rows, units)
    owned_hidden = local_hidden[0, 0]
    owned_gradients = local_grads[0, 0]

    held = []
    for step in range(N_X):
        start = lax.rem(x + step, N_X) * span
        block = lax.dynamic_slice_in_dim(owned_gradients, start, span, axis=1)
        held.append(jnp.concatenate([block, hidden, owned_hidden], axis=1))
    for step in (2, 1, 3):
        held[step] = lax.ppermute(
            held[step], "x", [(i, (i + step) % N_X) for i in range(N_X)]
        )

    blocks = column_blocks(arrived.reshape(-1, features), span)
    held, _ = lax.optimization_barrier((held, blocks))
    gathered = lax.all_to_all(blocks, ("x", "y_low"), 0, 0, tiled=True)
    gathered = gathered.reshape(-1, span)

    def by_core(rows_of_units):
        split = rows_of_units.reshape(-1, units // (2 * OWNED), 2, OWNED)
        return split.transpose(0, 2, 1, 3).reshape(-1, units)

    back = jnp.stack([block[:, span : span + units] for block in held[::-1]])
    twice = jnp.concatenate([back, back])
    routed = lax.dynamic_slice_in_dim(twice, N_X - 1 - x, N_X, axis=0).reshape(-1, units)
    routed = by_core(routed)
    owned = by_core(jnp.concatenate([block[:, span + units :] for block in held]))
    columns = jnp.concatenate([block[:, :span] for block in held])

    def partial_of(which):
        start = which * share
        return contract_rows(
            lax.dynamic_slice_in_dim(owned, start, share, axis=1), columns
        ) + contract_rows(lax.dynamic_slice_in_dim(routed, start, share, axis=1), gathered)

    other = partial_of(1 - core).astype(jnp.bfloat16)
    other = lax.ppermute(other, "core", [(0, 1), (1, 0)])
    partial = partial_of(core) + other.astype(jnp.float32)

    partial = partial.astype(jnp.bfloat16).reshape(2 * N_X, OWNED, span)
    partial = lax.all_to_all(partial, ("y_hi", "x"), 0, 0, tiled=True)
    return adamw(partial, weight, moment, second)


def solution(mesh):
    dp = ("y_hi", "x", "core")
    expert = ("z", "y_half", "y_low")
    fine = Mesh(mesh.devices.reshape(2, N_X, 2, 16, 2, 2), AXES)
    outs = P(expert, dp, None)
    return jax.shard_map(
        on_device,
        mesh=fine,
        in_specs=(
            P(dp, expert, None, None),
            P(dp, expert, None, None, None),
            P(dp, expert, None, None),
            P(dp, expert, None, None),
            P(dp, None, None),
            outs,
            outs,
            outs,
        ),
        out_specs=(outs, outs, outs),
        check_vma=False,
    )
```

```python
import jax
import jax.numpy as jnp
from jax import lax
from jax.experimental import pallas as pl
from jax.experimental.pallas import tpu as pltpu
from jax.sharding import Mesh, PartitionSpec as P

AXES = ("y_hi", "x", "core", "z", "y_half", "y_low")
N_X = 4
OWNED = 32
KERNEL_VMEM = 8 * 2**20

beta_one = 0.9
beta_two = 0.95
learn_rate = 0.00022
decay_rate = 0.1
epsilon = 1e-08
correct_one = 1.0 - 0.9**20
correct_two = 1.0 - 0.95**20


def contract_rows(left_rows, right_rows):
    return lax.dot_general(
        left_rows, right_rows, (((0,), (0,)), ((), ())), preferred_element_type=jnp.float32
    )


def column_blocks(near, span):
    rows = near.shape[0]

    def kernel(near_ref, out_ref, sems):
        copies = [
            pltpu.make_async_copy(
                near_ref.at[:, i * span : (i + 1) * span], out_ref.at[2 * i + j], sems.at[i, j]
            )
            for i in range(N_X)
            for j in range(2)
        ]
        for copy in copies:
            copy.start()
        for copy in copies:
            copy.wait()

    return pl.pallas_call(
        kernel,
        out_shape=jax.ShapeDtypeStruct((2 * N_X, rows, span), near.dtype),
        in_specs=[pl.BlockSpec(memory_space=pltpu.VMEM)],
        out_specs=pl.BlockSpec(memory_space=pl.ANY),
        scratch_shapes=[pltpu.SemaphoreType.DMA((N_X, 2))],
        compiler_params=pltpu.CompilerParams(vmem_limit_bytes=KERNEL_VMEM),
    )(near)


def unpacked(held, span, units):
    rows = held[0].shape[0]

    def kernel(*refs):
        blocks, (columns, routed, owned), sems = refs[:N_X], refs[N_X : N_X + 3], refs[-1]
        x = lax.axis_index("x")
        copies = []
        for step, block in enumerate(blocks):
            here = lax.rem(x + N_X - step, N_X)
            parts = (
                (block.at[:, :span], columns.at[step]),
                (block.at[:, span : span + units], routed.at[here]),
                (block.at[:, span + units :], owned.at[step]),
            )
            for j, (source, target) in enumerate(parts):
                copies.append(pltpu.make_async_copy(source, target, sems.at[step, j]))
                copies[-1].start()
        for copy in copies:
            copy.wait()

    outs = pl.pallas_call(
        kernel,
        out_shape=tuple(
            jax.ShapeDtypeStruct((N_X, rows, n), held[0].dtype) for n in (span, units, units)
        ),
        in_specs=[pl.BlockSpec(memory_space=pl.ANY)] * N_X,
        out_specs=(pl.BlockSpec(memory_space=pl.ANY),) * 3,
        scratch_shapes=[pltpu.SemaphoreType.DMA((N_X, 3))],
        compiler_params=pltpu.CompilerParams(vmem_limit_bytes=KERNEL_VMEM),
        cost_estimate=pl.CostEstimate(flops=2 * 10**10, bytes_accessed=2**21, transcendentals=0),
    )(*held)
    return tuple(out.reshape(N_X * rows, -1) for out in outs)


def adamw(sums, weight, moment, second):
    span = sums.shape[-1]

    rows = weight.shape[1]

    def kernel(sums_ref, weight_ref, moment_ref, second_ref, *rest):
        outs, held, sems = rest[:3], rest[3:6], rest[6]
        copies = []
        for i in range(N_X):
            cols = slice(i * span, (i + 1) * span)
            summed = sums_ref[i].astype(jnp.float32) + sums_ref[N_X + i].astype(jnp.float32)
            first = beta_one * moment_ref[0, :, cols].astype(jnp.float32)
            first = first + (1.0 - beta_one) * summed
            next_ = beta_two * second_ref[0, :, cols].astype(jnp.float32)
            next_ = next_ + (1.0 - beta_two) * summed * summed
            root = jnp.sqrt(next_ * (1.0 / correct_two)) + epsilon
            direction = first * (1.0 / correct_one) / root
            master = weight_ref[0, :, cols]
            held[0][i] = master - learn_rate * (direction + decay_rate * master)
            held[1][i] = first.astype(jnp.bfloat16)
            held[2][i] = next_.astype(jnp.bfloat16)
            for j in range(3):
                copies.append(
                    pltpu.make_async_copy(held[j].at[i], outs[j].at[0, :, cols], sems.at[j, i])
                )
                copies[-1].start()
        for copy in copies:
            copy.wait()

    arrays = (weight, moment, second)
    return pl.pallas_call(
        kernel,
        out_shape=tuple(jax.ShapeDtypeStruct(a.shape, a.dtype) for a in arrays),
        in_specs=[pl.BlockSpec(memory_space=pltpu.VMEM)] * 4,
        out_specs=(pl.BlockSpec(memory_space=pl.ANY),) * 3,
        scratch_shapes=[pltpu.VMEM((N_X, rows, span), a.dtype) for a in arrays]
        + [pltpu.SemaphoreType.DMA((3, N_X))],
        compiler_params=pltpu.CompilerParams(vmem_limit_bytes=KERNEL_VMEM),
    )(sums, *arrays)


def on_device(
    hidden_acts, token_gradients, local_hidden, local_grads, counts, weight, moment, second
):
    x = lax.axis_index("x")
    core = lax.axis_index("core")
    expert_id = lax.axis_index("z") * 2 + lax.axis_index("y_half")
    outgoing = token_gradients[0, 0]
    slots, features = outgoing.shape[1:]
    hidden = hidden_acts[0, 0]
    rows, units = hidden.shape
    span = features // N_X
    share = units // 2

    arrived = lax.all_to_all(outgoing, ("z", "y_half"), 0, 0, tiled=True)

    filled = lax.dynamic_index_in_dim(counts[0], expert_id, axis=1, keepdims=False)
    slot_ids = jnp.arange(slots, dtype=jnp.int32)
    is_live = (slot_ids[None, :] < filled[:, None]).reshape(rows)
    hidden = jnp.where(is_live[:, None], hidden, jnp.zeros_like(hidden))
    hidden = hidden.reshape(-1, 2, slots, units).transpose(1, 0, 2, 3).reshape(rows, units)
    both = jnp.concatenate([hidden, local_hidden[0, 0]]).reshape(2, rows, -1, 2, OWNED)
    hidden, owned_hidden = both.transpose(0, 1, 3, 2, 4).reshape(2, rows, units)
    owned_gradients = local_grads[0, 0]

    held = []
    for step in range(N_X):
        start = lax.rem(x + step, N_X) * span
        block = lax.dynamic_slice_in_dim(owned_gradients, start, span, axis=1)
        held.append(jnp.concatenate([block, hidden, owned_hidden], axis=1))
    for step in (2, 1, 3):
        held[step] = lax.ppermute(
            held[step], "x", [(i, (i + step) % N_X) for i in range(N_X)]
        )

    blocks = column_blocks(arrived.reshape(-1, features), span)
    held, _ = lax.optimization_barrier((held, blocks))
    gathered = lax.all_to_all(blocks, ("x", "y_low"), 0, 0, tiled=True)
    gathered = gathered.reshape(-1, span)

    columns, routed, owned = unpacked(held, span, units)

    local = contract_rows(owned, columns)

    def partial_of(which):
        start = which * share
        return lax.dynamic_slice_in_dim(local, start, share, axis=0) + contract_rows(
            lax.dynamic_slice_in_dim(routed, start, share, axis=1), gathered
        )

    other = partial_of(1 - core).astype(jnp.bfloat16)
    other = lax.ppermute(other, "core", [(0, 1), (1, 0)])
    partial = partial_of(core) + other.astype(jnp.float32)

    partial = partial.astype(jnp.bfloat16).reshape(2 * N_X, OWNED, span)
    partial = lax.all_to_all(partial, ("y_hi", "x"), 0, 0, tiled=True)
    return adamw(partial, weight, moment, second)


def solution(mesh):
    dp = ("y_hi", "x", "core")
    expert = ("z", "y_half", "y_low")
    fine = Mesh(mesh.devices.reshape(2, N_X, 2, 16, 2, 2), AXES)
    outs = P(expert, dp, None)
    return jax.shard_map(
        on_device,
        mesh=fine,
        in_specs=(
            P(dp, expert, None, None),
            P(dp, expert, None, None, None),
            P(dp, expert, None, None),
            P(dp, expert, None, None),
            P(dp, None, None),
            outs,
            outs,
            outs,
        ),
        out_specs=(outs, outs, outs),
        check_vma=False,
    )
```

```python
import jax
import jax.numpy as jnp
from jax import lax
from jax.experimental import pallas as pl
from jax.experimental.pallas import tpu as pltpu
from jax.sharding import Mesh, PartitionSpec as P

AXES = ("y_hi", "x", "core", "z_hi", "z_lo", "y_half", "y_low")
N_X = 4
OWNED = 32
KERNEL_VMEM = 8 * 2**20

beta_one = 0.9
beta_two = 0.95
learn_rate = 0.00022
decay_rate = 0.1
epsilon = 1e-08
correct_one = 1.0 - 0.9**20
correct_two = 1.0 - 0.95**20


def contract_rows(left_rows, right_rows):
    return lax.dot_general(
        left_rows, right_rows, (((0,), (0,)), ((), ())), preferred_element_type=jnp.float32
    )


def column_blocks(near, span):
    rows = near.shape[1]

    def kernel(near_ref, out_ref):
        for i in range(N_X):
            for k in range(2):
                block = near_ref[k, :, i * span : (i + 1) * span]
                for j in range(2):
                    out_ref[4 * i + 2 * k + j] = block

    return pl.pallas_call(
        kernel,
        out_shape=jax.ShapeDtypeStruct((4 * N_X, rows, span), near.dtype),
        in_specs=[pl.BlockSpec(memory_space=pltpu.VMEM)],
        out_specs=pl.BlockSpec(memory_space=pltpu.VMEM),
        compiler_params=pltpu.CompilerParams(vmem_limit_bytes=KERNEL_VMEM),
    )(near)


def unpacked(held, span, units):
    rows = held[0].shape[0]

    def kernel(*refs):
        blocks, (columns, routed, owned), sems = refs[:N_X], refs[N_X : N_X + 3], refs[-1]
        x = lax.axis_index("x")
        copies = []
        for step, block in enumerate(blocks):
            here = lax.rem(x + N_X - step, N_X)
            parts = (
                (block.at[:, :span], columns.at[step]),
                (block.at[:, span : span + units], routed.at[here]),
                (block.at[:, span + units :], owned.at[step]),
            )
            for j, (source, target) in enumerate(parts):
                copies.append(pltpu.make_async_copy(source, target, sems.at[step, j]))
                copies[-1].start()
        for copy in copies:
            copy.wait()

    outs = pl.pallas_call(
        kernel,
        out_shape=tuple(
            jax.ShapeDtypeStruct((N_X, rows, n), held[0].dtype) for n in (span, units, units)
        ),
        in_specs=[pl.BlockSpec(memory_space=pl.ANY)] * N_X,
        out_specs=(pl.BlockSpec(memory_space=pl.ANY),) * 3,
        scratch_shapes=[pltpu.SemaphoreType.DMA((N_X, 3))],
        compiler_params=pltpu.CompilerParams(vmem_limit_bytes=KERNEL_VMEM),
        cost_estimate=pl.CostEstimate(flops=6 * 10**10, bytes_accessed=2**21, transcendentals=0),
    )(*held)
    return tuple(out.reshape(N_X * rows, -1) for out in outs)


def adamw(sums, weight, moment, second):
    span = sums.shape[-1]

    rows = weight.shape[1]

    def kernel(sums_ref, weight_ref, moment_ref, second_ref, *rest):
        outs, held, sems = rest[:3], rest[3:6], rest[6]
        copies = []
        for i in range(N_X):
            cols = slice(i * span, (i + 1) * span)
            summed = sums_ref[i].astype(jnp.float32) + sums_ref[N_X + i].astype(jnp.float32)
            first = beta_one * moment_ref[0, :, cols].astype(jnp.float32)
            first = first + (1.0 - beta_one) * summed
            next_ = beta_two * second_ref[0, :, cols].astype(jnp.float32)
            next_ = next_ + (1.0 - beta_two) * summed * summed
            root = jnp.sqrt(next_ * (1.0 / correct_two)) + epsilon
            direction = first * (1.0 / correct_one) / root
            master = weight_ref[0, :, cols]
            held[0][i] = master - learn_rate * (direction + decay_rate * master)
            held[1][i] = first.astype(jnp.bfloat16)
            held[2][i] = next_.astype(jnp.bfloat16)
            for j in range(3):
                copies.append(
                    pltpu.make_async_copy(held[j].at[i], outs[j].at[0, :, cols], sems.at[j, i])
                )
                copies[-1].start()
        for copy in copies:
            copy.wait()

    arrays = (weight, moment, second)
    return pl.pallas_call(
        kernel,
        out_shape=tuple(jax.ShapeDtypeStruct(a.shape, a.dtype) for a in arrays),
        in_specs=[pl.BlockSpec(memory_space=pltpu.VMEM)] * 4,
        out_specs=(pl.BlockSpec(memory_space=pl.ANY),) * 3,
        scratch_shapes=[pltpu.VMEM((N_X, rows, span), a.dtype) for a in arrays]
        + [pltpu.SemaphoreType.DMA((3, N_X))],
        compiler_params=pltpu.CompilerParams(vmem_limit_bytes=KERNEL_VMEM),
    )(sums, *arrays)


def on_device(
    hidden_acts, token_gradients, local_hidden, local_grads, counts, weight, moment, second
):
    x = lax.axis_index("x")
    core = lax.axis_index("core")
    expert_id = lax.axis_index(("z_hi", "z_lo", "y_half"))
    outgoing = token_gradients[0, 0]
    slots, features = outgoing.shape[1:]
    hidden = hidden_acts[0, 0]
    rows, units = hidden.shape
    span = features // N_X
    share = units // 2

    outgoing = outgoing.reshape(-1, 2, 2, slots, features).transpose(0, 2, 1, 3, 4)
    outgoing = outgoing.reshape(-1, 2, slots, features)
    arrived = lax.all_to_all(outgoing, ("z_hi", "y_half"), 0, 0, tiled=True)

    filled = lax.dynamic_index_in_dim(counts[0], expert_id, axis=1, keepdims=False)
    slot_ids = jnp.arange(slots, dtype=jnp.int32)
    is_live = (slot_ids[None, :] < filled[:, None]).reshape(rows)
    hidden = jnp.where(is_live[:, None], hidden, jnp.zeros_like(hidden))
    hidden = hidden.reshape(-1, 2, 2, 2, slots, units).transpose(1, 3, 0, 2, 4, 5)
    hidden = hidden.reshape(rows, units)
    both = jnp.concatenate([hidden, local_hidden[0, 0]]).reshape(2, rows, -1, 2, OWNED)
    hidden, owned_hidden = both.transpose(0, 1, 3, 2, 4).reshape(2, rows, units)
    owned_gradients = local_grads[0, 0]

    held = []
    for step in range(N_X):
        start = lax.rem(x + step, N_X) * span
        block = lax.dynamic_slice_in_dim(owned_gradients, start, span, axis=1)
        held.append(jnp.concatenate([block, hidden, owned_hidden], axis=1))
    for step in (2, 1, 3):
        held[step] = lax.ppermute(
            held[step], "x", [(i, (i + step) % N_X) for i in range(N_X)]
        )

    near = arrived.transpose(1, 0, 2, 3).reshape(2, -1, features)
    blocks = column_blocks(near, span)
    held, _ = lax.optimization_barrier((held, blocks))
    gathered = lax.all_to_all(blocks, ("x", "z_lo", "y_low"), 0, 0, tiled=True)
    gathered = gathered.reshape(-1, span)

    columns, routed, owned = unpacked(held, span, units)

    def partial_of(which):
        start = which * share
        return contract_rows(
            lax.dynamic_slice_in_dim(owned, start, share, axis=1), columns
        ) + contract_rows(lax.dynamic_slice_in_dim(routed, start, share, axis=1), gathered)

    other = partial_of(1 - core).astype(jnp.bfloat16)
    other = lax.ppermute(other, "core", [(0, 1), (1, 0)])
    partial = partial_of(core) + other.astype(jnp.float32)

    partial = partial.astype(jnp.bfloat16).reshape(2 * N_X, OWNED, span)
    partial = lax.all_to_all(partial, ("y_hi", "x"), 0, 0, tiled=True)
    return adamw(partial, weight, moment, second)


def solution(mesh):
    dp = ("y_hi", "x", "core")
    expert = ("z_hi", "z_lo", "y_half", "y_low")
    fine = Mesh(mesh.devices.reshape(2, N_X, 2, 8, 2, 2, 2), AXES)
    outs = P(expert, dp, None)
    return jax.shard_map(
        on_device,
        mesh=fine,
        in_specs=(
            P(dp, expert, None, None),
            P(dp, expert, None, None, None),
            P(dp, expert, None, None),
            P(dp, expert, None, None),
            P(dp, None, None),
            outs,
            outs,
            outs,
        ),
        out_specs=(outs, outs, outs),
        check_vma=False,
    )
```
